128 devices in a mesh: dp: 8 (over x, y_lo), fsdp: 16 (over y_hi, z, core).
Axes of the slice: x: 4, y: 4 (y_hi: 2, y_lo: 2; y = y_hi * 2 + y_lo), z: 4, core: 2. Of those that a mesh axis runs over, the one named last changes fastest.
Arguments:
- tokens: float32 [131072, 4096], P(('dp', 'fsdp')), may hold values from -6 to 6
- curvature: float32 [131072, 512], P(('dp', 'fsdp')), may hold values from 0.05 to 1
- values: float32 [4096, 512], P('fsdp'), may hold values from -6 to 6
- input_basis: float32 [4096, 4096], P(None, ('dp', 'fsdp')), may hold values from -1 to 1, as said below
- output_basis: float32 [512, 512], replicated, may hold values from -1 to 1, as said below
- eigenvalues: float32 [4096, 512], P(('dp', 'fsdp')), may hold values from 0.3 to 3
Outputs:
- stepped: float32 [4096, 512], P('fsdp')
The draws below stay inside these ranges and needn't reach their ends.
Inputs may be any that keep to these rules, and one draw needn't show every extreme that they name: `input_basis`: an orthogonal 4096 x 4096 matrix. `output_basis`: an orthogonal 512 x 512 matrix.
All inputs are finite; a program needn't handle non-finite values.
Results may differ from the reference program's by a relative error of at most 0.000071.
Values sent between devices are 32-bit elements; how exact they have to be, the bound alone decides.
A program may use at most 128 MiB of HBM per device.

```python
import math
import jax
import jax.numpy as jnp
from jax import lax

D = 4096
KV = 512
TOKENS = 131072


def draw_input_basis(key, part):
    matrix = jax.random.normal(jax.random.fold_in(key, 11), (D, D), jnp.float32)
    orthogonal, upper = jnp.linalg.qr(matrix)
    return orthogonal


def draw_output_basis(key, part):
    matrix = jax.random.normal(jax.random.fold_in(key, 23), (KV, KV), jnp.float32)
    orthogonal, upper = jnp.linalg.qr(matrix)
    return orthogonal


def levels(own_key, dims, split, least, top_value):
    factor_of = 1.0
    for position, shards_of in split:
        heights = jax.random.uniform(jax.random.fold_in(jax.random.fold_in(own_key, 6), position), (shards_of,), jnp.float32, least / len(split), top_value / len(split))
        factor_of = factor_of * jnp.repeat(jnp.exp(heights), dims[position] // shards_of).reshape((-1,) + (1,) * (len(dims) - 1 - position))
    return factor_of


def centred(own_key, dims, spread, bound, cuts=(), dtype=jnp.bfloat16):
    values = spread * jax.random.normal(own_key, dims, jnp.float32)
    if cuts:
        values = values * levels(own_key, dims, cuts, -0.22, 0.18)
    return jnp.clip(values, -bound, bound).astype(dtype)


def setup_inputs(seed: int = 0) -> dict:
    seeds = jax.random.split(jax.random.key(seed), 7)
    return {
        "tokens": centred(seeds[0], (TOKENS, D), 1.0, 6.0, ((0, 128),), jnp.float32),
        "curvature": jnp.clip(jnp.exp(math.log(1.0) - 2.9957323 * jax.random.uniform(seeds[1], (TOKENS, KV), jnp.float32) ** levels(seeds[1], (TOKENS, KV), ((0, 128),), -0.2, 0.2)), 0.05, 1.0),
        "values": centred(seeds[2], (D, KV), 1.0, 6.0, ((0, 16),), jnp.float32),
        "input_basis": draw_input_basis(jax.random.fold_in(seeds[6], 71), 0),
        "output_basis": draw_output_basis(jax.random.fold_in(seeds[6], 71), 0),
        "eigenvalues": jnp.clip(jnp.exp(math.log(3.0) - 2.3025851 * jax.random.uniform(seeds[5], (D, KV), jnp.float32) ** levels(seeds[5], (D, KV), ((0, 128),), -0.2, 0.2)), 0.3, 3.0),
    }


def reference(tokens, curvature, values, input_basis, output_basis, eigenvalues):
    highest = lax.Precision.HIGHEST
    projected = jnp.dot(tokens.astype(jnp.float32), values.astype(jnp.float32), precision=highest, preferred_element_type=jnp.float32)
    weighted = curvature * projected
    moment = jnp.dot(tokens.T.astype(jnp.float32), weighted.astype(jnp.float32), precision=highest, preferred_element_type=jnp.float32) / TOKENS
    rotated = jnp.dot(jnp.dot(input_basis.T.astype(jnp.float32), moment.astype(jnp.float32), precision=highest, preferred_element_type=jnp.float32).astype(jnp.float32), output_basis.astype(jnp.float32), precision=highest, preferred_element_type=jnp.float32)
    scaled = rotated / eigenvalues
    update = jnp.dot(jnp.dot(input_basis.astype(jnp.float32), scaled.astype(jnp.float32), precision=highest, preferred_element_type=jnp.float32).astype(jnp.float32), output_basis.T.astype(jnp.float32), precision=highest, preferred_element_type=jnp.float32)
    return values - update
```

```python
import functools

import jax
import jax.numpy as jnp
from jax import lax
from jax.experimental import pallas as pl
from jax.experimental.pallas import tpu as pltpu
from jax.sharding import PartitionSpec as P

F32 = jnp.float32
BF16 = jnp.bfloat16
MESH = pl.DeviceIdType.MESH
ALL = slice(None)

ORDERS = (("z", "y", "x"), ("y", "x", "z"), ("x", "z", "y"))
ROWS = ((0, 24), (24, 48), (48, 64))


def split(v):
    hi = v.astype(BF16)
    return hi, (v - hi.astype(F32)).astype(BF16)


def mm(a, b, dims=(((1,), (0,)), ((), ()))):
    return lax.dot_general(a, b, dims, preferred_element_type=F32)


NT = (((1,), (1,)), ((), ()))


def mm3(ah, al, bh, bl, dims=(((1,), (0,)), ((), ()))):
    return mm(ah, bh, dims) + (mm(ah, bl, dims) + mm(al, bh, dims))


def half_shape(o, p):
    lo, hi = ROWS[o]
    rows = hi - lo
    r_axis = ORDERS[o][2]
    if p == 2:
        return (16, 128)
    if p == 1:
        return (2, rows, 128)
    q_axis = ORDERS[o][1]
    dims = [a for a in "zyx" if a in (q_axis, r_axis)]
    return tuple(2 if a == r_axis else 4 for a in dims) + (rows, 128)


def full_shape(o, p):
    lo, hi = ROWS[o]
    return ((4, 4), (4,), ())[p] + (hi - lo, 128)


def kernel(tok, curv, val, ut, ot, outb, eig, out, *scr, inverse_total):
    (V, thi, tlo, stage, cv, acc, whi, wlo, zhi, zlo, sib, mg, utg, uhi, ulo, eg, ub, ubr, rb, ud,
     *rest) = scr
    RH = [[rest[o * 3 + p] for p in range(3)] for o in range(3)]
    RF = [[rest[9 + o * 3 + p] for p in range(3)] for o in range(3)]
    (ag_s, ag_r, fw_s, fw_r, u_s, u_r, e_s, e_r, sb_s, sb_r, rs_s, rs_r,
     mg_s, mg_r, ub_s, ub_r, ud_s, ud_r, st_sem, lc_sem) = rest[18:]

    dp = lax.axis_index("dp")
    fs = lax.axis_index("fsdp")
    x, ylo = lax.div(dp, 2), lax.rem(dp, 2)
    yhi, z, c = lax.div(fs, 8), lax.rem(lax.div(fs, 2), 4), lax.rem(fs, 2)
    y = yhi * 2 + ylo
    pos = {"x": x, "y": y, "z": z}

    def dev(x_, y_, z_, c_):
        return (x_ * 2 + lax.rem(y_, 2), lax.div(y_, 2) * 8 + z_ * 2 + c_)

    def off(v, d):
        return lax.rem(v + (d + 4), 4)

    def nb(axis, d):
        q = dict(pos)
        q[axis] = off(q[axis], d)
        return dev(q["x"], q["y"], q["z"], c)

    sibling = dev(x, y, z, 1 - c)

    def rc(src, dst, ss, rs, to):
        return pltpu.make_async_remote_copy(
            src_ref=src, dst_ref=dst, send_sem=ss, recv_sem=rs, device_id=to, device_id_type=MESH)

    def block_index(o, axis_idx, rows):
        lo, hi = ROWS[o]
        if rows is None:
            rows = (lo, hi)
        return (axis_idx["z"], axis_idx["y"], axis_idx["x"], slice(*rows))

    def grid_index(o, lead, k, half):
        axes = ORDERS[o]
        idx = {a: pos[a] for a in axes[:lead]}
        idx[axes[lead]] = k
        for a in axes[lead + 1:]:
            idx[a] = ALL
        rows = None
        if half is not None:
            if lead == 2:
                lo, hi = ROWS[o]
                mid = lo + (16 if hi - lo == 24 else 8)
                rows = (lo, mid) if half == 0 else (mid, hi)
            else:
                idx[axes[2]] = slice(0, 2) if half == 0 else slice(2, 4)
        return block_index(o, idx, rows)

    def vidx(r, cc, g):
        return (r, g[0], cc, g[1], g[2], g[3], ALL)

    def ag_copy(r, o, p, k):
        lead = 2 - p
        axis = ORDERS[o][lead]
        me = pos[axis]
        i = ((r * 3 + o) * 3 + p) * 4 + k
        if k == 0:
            g, to = grid_index(o, lead, me, None), nb(axis, 1)
        elif k == 1:
            g, to = grid_index(o, lead, me, None), nb(axis, -1)
        elif k == 2:
            g, to = grid_index(o, lead, off(me, -1), 0), nb(axis, 1)
        else:
            g, to = grid_index(o, lead, off(me, 1), 1), nb(axis, -1)
        ref = V.at[vidx(r, c, g)]
        return rc(ref, ref, ag_s.at[i], ag_r.at[i], to)

    def fw_copy(r, o, d):
        me = pos[ORDERS[o][0]]
        ref = V.at[vidx(r, c, grid_index(o, 0, off(me, d), None))]
        i = (r * 3 + o) * 4 + (d + 4) % 4
        return rc(ref, ref, fw_s.at[i], fw_r.at[i], sibling)

    def ag_start(r, p):
        for o in range(3):
            ag_copy(r, o, p, 0).start()
            ag_copy(r, o, p, 1).start()
            if p == 2:
                fw_copy(r, o, 0).start()

    def ag_relay(r, p):
        for o in range(3):
            ag_copy(r, o, p, 0).wait_recv()
            ag_copy(r, o, p, 2).start()
            ag_copy(r, o, p, 1).wait_recv()
            ag_copy(r, o, p, 3).start()
            if p == 2:
                fw_copy(r, o, -1).start()
                fw_copy(r, o, 1).start()

    def ag_finish(r, p):
        for o in range(3):
            ag_copy(r, o, p, 2).wait_recv()
            ag_copy(r, o, p, 3).wait_recv()
            if p == 2:
                fw_copy(r, o, 2).start()

    def fw_wait(r):
        for o in range(3):
            for d in (0, -1, 1, 2):
                fw_copy(r, o, d).wait_recv()

    def ag_sent(r):
        for o in range(3):
            for p in range(3):
                for k in range(4):
                    ag_copy(r, o, p, k).wait_send()
            for d in (0, -1, 1, 2):
                fw_copy(r, o, d).wait_send()

    def u_copy(k):
        i, to, rows = ((x, nb("x", 1), ALL), (x, nb("x", -1), ALL),
                       (off(x, -1), nb("x", 1), slice(0, 16)), (off(x, 1), nb("x", -1), slice(16, 32)))[k]
        ref = utg.at[i, rows, :]
        return rc(ref, ref, u_s.at[k], u_r.at[k], to)

    def e_copy(d):
        xt = off(x, d)
        cols = pl.ds(pl.multiple_of(xt * 128, 128), 128)
        return rc(eig.at[:, cols], eg.at[x], e_s.at[d - 1], e_r.at[d - 1], dev(xt, y, z, c))

    def sb_copy(s, zi):
        return rc(V.at[s, zi, 1 - c], sib.at[s, zi], sb_s.at[s * 4 + zi], sb_r.at[s * 4 + zi], sibling)

    def rh_view(s, o, p, d):
        ref = RH[o][p]
        if p == 2:
            lo, hi = ROWS[o]
            first = 16 if hi - lo == 24 else 8
            n = first if d == 0 else hi - lo - first
            return (s, d, slice(0, n), ALL), ref
        return (s, d), ref

    def rs_copy(s, o, p, k):
        axis = ORDERS[o][p]
        me = pos[axis]
        i = ((s * 3 + o) * 3 + p) * 4 + k
        d = k % 2
        to = nb(axis, 1 if d == 0 else -1)
        if k < 2:
            g = grid_index(o, p, off(me, 2), d)
            idx, ref = rh_view(s, o, p, d)
            dst = ref.at[idx]
        else:
            g = grid_index(o, p, off(me, 1 if d == 0 else -1), None)
            dst = RF[o][p].at[s, d]
        return rc(V.at[vidx(s, c, g)], dst, rs_s.at[i], rs_r.at[i], to)

    def rs_start(s, p):
        for o in range(3):
            rs_copy(s, o, p, 0).start()
            rs_copy(s, o, p, 1).start()

    def rs_mid(s, p):
        for o in range(3):
            me = pos[ORDERS[o][p]]
            for d, k in ((0, off(me, 1)), (1, off(me, -1))):
                rs_copy(s, o, p, d).wait_recv()
                idx, ref = rh_view(s, o, p, d)
                v = vidx(s, c, grid_index(o, p, k, d))
                V[v] = V[v] + ref[idx]
                rs_copy(s, o, p, 2 + d).start()

    def rs_end(s, p):
        for o in range(3):
            me = pos[ORDERS[o][p]]
            rs_copy(s, o, p, 2).wait_recv()
            rs_copy(s, o, p, 3).wait_recv()
            v = vidx(s, c, grid_index(o, p, me, None))
            V[v] = V[v] + (RF[o][p][s, 0] + RF[o][p][s, 1])

    def sib_add(s):
        def one(zi, _):
            sb_copy(s, zi).wait_recv()
            for yi in range(4):
                V[s, zi, c, yi] = V[s, zi, c, yi] + sib[s, zi, yi]
            return 0
        lax.fori_loop(0, 4, one, 0)

    def peer(k):
        return off(y, 0 + lax.div(k, 4)), off(z, 0 + lax.rem(k, 4))

    def mg_copy(s, k):
        yt, zt = peer(k)
        i = s * 16 + k
        return rc(V.at[s, z, c, y, x], mg.at[s, c, y, z], mg_s.at[i], mg_r.at[i], dev(x, yt, zt, c))

    def mg_fwd(s):
        return rc(mg.at[s, c], mg.at[s, c], mg_s.at[s * 16], mg_r.at[s * 16], sibling)

    def ub_copy(s, k):
        yt, zt = peer(k)
        i = s * 16 + k
        return rc(ub.at[s, c, yt, zt], rb.at[s, k], ub_s.at[i], ub_r.at[i], dev(x, yt, zt, c))

    def ub_sib(s):
        return rc(ub.at[s, 1 - c], ubr.at[s], ub_s.at[s * 16], ub_r.at[s * 16], sibling)

    def ud_copy(s, k):
        xt = off(x, lax.div(k, 2))
        lt = lax.rem(ylo + lax.rem(k, 2), 2)
        i = s * 8 + k
        return rc(ud.at[s, x, ylo], ud.at[s, x, ylo], ud_s.at[i], ud_r.at[i], dev(xt, yhi * 2 + lt, z, c))

    def loop(lo, hi, f):
        def step(i, carry):
            f(i)
            return carry
        lax.fori_loop(lo, hi, step, 0)

    def t_copy(j, slot):
        cols = pl.ds(pl.multiple_of(j * 256, 256), 256)
        return pltpu.make_async_copy(tok.at[:, cols], stage.at[slot], st_sem.at[slot])

    t_copy(0, 0).start()
    t_copy(1, 1).start()
    own = []
    for yl in range(2):
        for r in range(2):
            pass
    val_copies = []
    rowbase = pl.multiple_of(x * 64, 64)
    colbase = pl.multiple_of(ylo * 128, 128)
    for r in range(2):
        cols = pl.ds(pl.multiple_of(colbase + r * 256, 128), 128)
        val_copies.append(pltpu.make_async_copy(
            val.at[pl.ds(rowbase, 64), cols], V.at[r, z, c, y, x], lc_sem.at[r]))
        val_copies[-1].start()
    cv_copy = pltpu.make_async_copy(curv, cv, lc_sem.at[2])
    cv_copy.start()
    ut_copy = pltpu.make_async_copy(ut, utg.at[x], lc_sem.at[3])
    ut_copy.start()

    barrier = pltpu.get_barrier_semaphore()
    loop(1, 16, lambda k: pl.semaphore_signal(
        barrier, inc=1, device_id=dev(x, *peer(k), c), device_id_type=MESH))

    def greet_dp(k):
        xt = off(x, lax.div(k, 2))
        lt = lax.rem(ylo + lax.rem(k, 2), 2)
        pl.semaphore_signal(barrier, inc=1, device_id=dev(xt, yhi * 2 + lt, z, c), device_id_type=MESH)
    loop(2, 8, greet_dp)
    pl.semaphore_signal(barrier, inc=1, device_id=sibling, device_id_type=MESH)
    pl.semaphore_wait(barrier, 22)

    for cp in val_copies:
        cp.wait()

    def split_block(j):
        slot = lax.rem(j, 2)
        t_copy(j, slot).wait()
        kb = lax.div(j, 2)
        cols = pl.ds(pl.multiple_of(lax.rem(j, 2) * 256, 256), 256)

        def rows(i):
            rr = pl.ds(pl.multiple_of(i * 256, 256), 256)
            h, l = split(stage[slot, rr, :])
            thi[kb, rr, cols] = h
            tlo[kb, rr, cols] = l
        loop(0, 4, rows)

        @pl.when(j < 14)
        def _():
            t_copy(j + 2, slot).start()

    ag_start(0, 0)
    ag_start(1, 0)
    loop(0, 2, split_block)
    ag_relay(0, 0)
    ag_relay(1, 0)
    loop(2, 4, split_block)
    ag_finish(0, 0)
    ag_start(0, 1)
    ag_finish(1, 0)
    ag_start(1, 1)
    loop(4, 7, split_block)
    ag_relay(0, 1)
    ag_relay(1, 1)
    loop(7, 9, split_block)
    ag_finish(0, 1)
    ag_start(0, 2)
    ag_finish(1, 1)
    loop(9, 14, split_block)
    ag_relay(0, 2)
    ag_start(1, 2)
    loop(14, 16, split_block)
    ag_finish(0, 2)
    ut_copy.wait()
    u_copy(0).start()
    u_copy(1).start()
    for d in (1, 2, 3):
        e_copy(d).start()
    eg[x] = eig[:, pl.ds(pl.multiple_of(x * 128, 128), 128)]
    cv_copy.wait()
    fw_wait(0)

    def project(r, steps):
        def body(kb):
            for at, fn in steps:
                pl.when(kb == at)(fn)
            yh, zi = lax.div(kb, 4), lax.rem(kb, 4)
            rows = []
            for ci in range(2):
                tiles = [V[r, zi, ci, yh * 2 + yl].reshape(256, 128) for yl in range(2)]
                rows.append(jnp.concatenate(tiles, axis=1))
            vh, vl = split(jnp.concatenate(rows, axis=0))
            for m in range(2):
                rr = slice(m * 512, (m + 1) * 512)
                part = mm3(thi[kb, rr, :], tlo[kb, rr, :], vh, vl)

                @pl.when(kb == 0)
                def _():
                    acc[rr, :] = part

                @pl.when(kb > 0)
                def _():
                    acc[rr, :] = acc[rr, :] + part
        loop(0, 8, body)

        def weigh(i):
            rr = pl.ds(pl.multiple_of(i * 256, 256), 256)
            cols = slice(r * 256, (r + 1) * 256)
            h, l = split(cv[rr, cols] * acc[rr, :] * inverse_total)
            whi[rr, cols] = h
            wlo[rr, cols] = l
        loop(0, 4, weigh)

    def u_relay():
        u_copy(0).wait_recv()
        u_copy(2).start()
        u_copy(1).wait_recv()
        u_copy(3).start()

    project(0, [(6, lambda: ag_relay(1, 2))])
    ag_finish(1, 2)
    fw_wait(1)
    project(1, [(6, u_relay)])
    ag_sent(0)
    ag_sent(1)

    for s in range(2):
        oh, ol = split(ot[:, s].reshape(256, 512))

        def z_part(i):
            rr = pl.ds(pl.multiple_of(i * 256, 256), 256)
            zz = mm3(oh, ol, whi[rr, :], wlo[rr, :], NT)
            h, l = split(zz)
            zhi[s, :, rr] = h
            zlo[s, :, rr] = l
        loop(0, 4, z_part)

    def moment(s, steps):
        def body(i):
            for at, fn in steps:
                pl.when(i == at)(fn)
            zi, yh = lax.div(i, 2), lax.rem(i, 2)
            kb = yh * 4 + zi
            mo = mm3(zhi[s], zlo[s], thi[kb], tlo[kb])
            for ci in range(2):
                for yl in range(2):
                    q = (ci * 2 + yl) * 128
                    V[s, zi, ci, yh * 2 + yl] = mo[:, q:q + 128].reshape(4, 64, 128)

            @pl.when(yh == 1)
            def _():
                sb_copy(s, zi).start()
        loop(0, 8, body)

    moment(0, [])

    def first():
        sib_add(0)
        rs_start(0, 0)

    moment(1, [(1, first), (4, lambda: rs_mid(0, 0)), (7, lambda: (rs_end(0, 0), rs_start(0, 1)) and None)])
    u_copy(2).wait_recv()
    u_copy(3).wait_recv()

    def mg_send(s):
        mg[s, c, y, z] = V[s, z, c, y, x]
        loop(1, 16, lambda k: mg_copy(s, k).start())

    def mg_wait(s):
        loop(1, 16, lambda k: mg_copy(s, k).wait_recv())
        mg_fwd(s).start()

    def rotate(s):
        mg_fwd(s).wait_recv()
        total = jnp.zeros((64, 128), F32)
        for kb in range(8):
            yh, zi = kb // 4, kb % 4
            lhs = jnp.concatenate([mg[s, ci, yh * 2 + yl, zi] for ci in range(2) for yl in range(2)], axis=1)
            lh, ll = split(lhs)
            cols = slice(kb * 512, (kb + 1) * 512)
            total = total + mm3(lh, ll, uhi[:, cols], ulo[:, cols], NT)
        et = eg[...].reshape(128, 128).T
        sh, sl = split(total / et[s * 64:(s + 1) * 64])
        for kb in range(8):
            yh, zi = kb // 4, kb % 4
            cols = slice(kb * 512, (kb + 1) * 512)
            part = mm3(sh, sl, uhi[:, cols], ulo[:, cols])
            for ci in range(2):
                for yl in range(2):
                    q = (ci * 2 + yl) * 128
                    ub[s, ci, yh * 2 + yl, zi] = part[:, q:q + 128]
        ub_sib(s).start()

    def ub_send(s):
        ub_sib(s).wait_recv()
        for yi in range(4):
            ub[s, c, yi] = ub[s, c, yi] + ubr[s, yi]
        loop(1, 16, lambda k: ub_copy(s, k).start())

    def ud_send(s):
        loop(1, 16, lambda k: ub_copy(s, k).wait_recv())
        total = ub[s, c, y, z]
        for k in range(1, 16):
            total = total + rb[s, k]
        ud[s, x, ylo] = total
        loop(1, 8, lambda k: ud_copy(s, k).start())

    sib_add(1)
    rs_start(1, 0)
    rs_mid(0, 1)
    for i in range(4):
        h, l = split(utg[i])
        uhi[i * 32:(i + 1) * 32, :] = h
        ulo[i * 32:(i + 1) * 32, :] = l
    for d in (1, 2, 3):
        e_copy(d).wait_recv()
    rs_end(0, 1)
    rs_start(0, 2)
    rs_mid(1, 0)
    rs_mid(0, 2)
    rs_end(0, 2)
    mg_send(0)
    rs_end(1, 0)
    rs_start(1, 1)
    mg_wait(0)
    rs_mid(1, 1)
    rs_end(1, 1)
    rs_start(1, 2)
    rotate(0)
    rs_mid(1, 2)
    rs_end(1, 2)
    mg_send(1)
    ub_send(0)
    mg_wait(1)
    rotate(1)
    ud_send(0)
    ub_send(1)
    oh, ol = split(outb[...])
    ud_send(1)
    loop(1, 8, lambda k: ud_copy(0, k).wait_recv())
    loop(1, 8, lambda k: ud_copy(1, k).wait_recv())
    cols = []
    for yl in range(2):
        cols.append(jnp.concatenate([ud[s, xi, yl] for xi in range(4) for s in range(2)], axis=0))
    dh, dl = split(jnp.concatenate(cols, axis=1))
    out[...] = mm3(oh, ol, dh, dl).T

    for k in range(4):
        u_copy(k).wait_send()
    for d in (1, 2, 3):
        e_copy(d).wait_send()
    for s in range(2):
        loop(0, 4, lambda zi: sb_copy(s, zi).wait_send())
        for o in range(3):
            for p in range(3):
                for k in range(4):
                    rs_copy(s, o, p, k).wait_send()
        mg_fwd(s).wait_send()
        ub_sib(s).wait_send()
        loop(1, 16, lambda k: mg_copy(s, k).wait_send())
        loop(1, 16, lambda k: ub_copy(s, k).wait_send())
        loop(1, 8, lambda k: ud_copy(s, k).wait_send())


def body(tokens, curvature, values, input_basis, output_basis, eigenvalues):
    inverse_total = 1.0 / (tokens.shape[0] * lax.axis_size("dp") * lax.axis_size("fsdp"))
    dma = pltpu.SemaphoreType.DMA
    scratch = [
        pltpu.VMEM((2, 4, 2, 4, 4, 64, 128), F32),
        pltpu.VMEM((8, 1024, 512), BF16),
        pltpu.VMEM((8, 1024, 512), BF16),
        pltpu.VMEM((2, 1024, 256), F32),
        pltpu.VMEM((1024, 512), F32),
        pltpu.VMEM((1024, 256), F32),
        pltpu.VMEM((1024, 512), BF16),
        pltpu.VMEM((1024, 512), BF16),
        pltpu.VMEM((2, 256, 1024), BF16),
        pltpu.VMEM((2, 256, 1024), BF16),
        pltpu.VMEM((2, 4, 4, 4, 64, 128), F32),
        pltpu.VMEM((2, 2, 4, 4, 64, 128), F32),
        pltpu.VMEM((4, 32, 4096), F32),
        pltpu.VMEM((128, 4096), BF16),
        pltpu.VMEM((128, 4096), BF16),
        pltpu.VMEM((4, 32, 128), F32),
        pltpu.VMEM((2, 2, 4, 4, 64, 128), F32),
        pltpu.VMEM((2, 4, 4, 64, 128), F32),
        pltpu.VMEM((2, 16, 64, 128), F32),
        pltpu.VMEM((2, 4, 2, 64, 128), F32),
    ]
    scratch += [pltpu.VMEM((2, 2) + half_shape(o, p), F32) for o in range(3) for p in range(3)]
    scratch += [pltpu.VMEM((2, 2) + full_shape(o, p), F32) for o in range(3) for p in range(3)]
    for n in (72, 72, 24, 24, 4, 4, 3, 3, 8, 8, 72, 72, 32, 32, 32, 32, 16, 16, 2, 4):
        scratch.append(dma((n,)))
    hbm = pl.BlockSpec(memory_space=pl.ANY)
    vmem = pl.BlockSpec(memory_space=pltpu.VMEM)
    update = pl.pallas_call(
        functools.partial(kernel, inverse_total=inverse_total),
        out_shape=jax.ShapeDtypeStruct((256, 512), F32),
        in_specs=[hbm, hbm, hbm, hbm, vmem, vmem, vmem],
        out_specs=vmem,
        scratch_shapes=scratch,
        compiler_params=pltpu.CompilerParams(
            collective_id=0, has_side_effects=True, vmem_limit_bytes=63 * 1024 * 1024
        ),
        cost_estimate=pl.CostEstimate(flops=30_000_000_000, bytes_accessed=24_000_000, transcendentals=0),
    )(
        tokens,
        curvature,
        values,
        input_basis.T,
        output_basis.T.reshape(4, 2, 64, 512),
        output_basis,
        eigenvalues,
    )
    return values - update


def solution(mesh):
    placed = (
        P(("dp", "fsdp"), None),
        P(("dp", "fsdp"), None),
        P("fsdp", None),
        P(None, ("dp", "fsdp")),
        P(),
        P(("dp", "fsdp"), None),
    )
    return jax.shard_map(
        body, mesh=mesh, in_specs=placed, out_specs=P("fsdp", None), check_vma=False
    )
```

```python
import functools

import jax
import jax.numpy as jnp
from jax import lax
from jax.experimental import pallas as pl
from jax.experimental.pallas import tpu as pltpu
from jax.sharding import PartitionSpec as P

F32 = jnp.float32
BF16 = jnp.bfloat16
MESH = pl.DeviceIdType.MESH
ALL = slice(None)

ORDERS = (("z", "y", "x"), ("y", "x", "z"), ("x", "z", "y"))
ROWS = ((0, 24), (24, 48), (48, 64))


def split(v):
    hi = v.astype(BF16)
    return hi, (v - hi.astype(F32)).astype(BF16)


def mm(a, b, dims=(((1,), (0,)), ((), ()))):
    return lax.dot_general(a, b, dims, preferred_element_type=F32)


NT = (((1,), (1,)), ((), ()))


def mm3(ah, al, bh, bl, dims=(((1,), (0,)), ((), ()))):
    return mm(ah, bh, dims) + (mm(ah, bl, dims) + mm(al, bh, dims))


def full_shape(o, p):
    lo, hi = ROWS[o]
    return ((4, 4), (4,), ())[p] + (hi - lo, 128)


def kernel(tok, curv, val, ut, outb_hbm, eig, out, *scr, inverse_total):
    (V, thi, tlo, stage, cv, acc, whi, wlo, zhi, zlo, sib, mg, utg, uhi, ulo, eg, et, ub, rb, us, ud,
     outb, oth, otl, *rest) = scr
    RF = [[rest[o * 3 + p] for p in range(3)] for o in range(3)]
    (ag_s, ag_r, fw_s, fw_r, u_s, u_r, e_s, e_r, sb_s, sb_r, rs_s, rs_r,
     mg_s, mg_r, ub_s, ub_r, ud_s, ud_r, st_sem, lc_sem) = rest[9:]

    dp = lax.axis_index("dp")
    fs = lax.axis_index("fsdp")
    x, ylo = lax.div(dp, 2), lax.rem(dp, 2)
    yhi, z, c = lax.div(fs, 8), lax.rem(lax.div(fs, 2), 4), lax.rem(fs, 2)
    y = yhi * 2 + ylo
    pos = {"x": x, "y": y, "z": z}

    def dev(x_, y_, z_, c_):
        return (x_ * 2 + lax.rem(y_, 2), lax.div(y_, 2) * 8 + z_ * 2 + c_)

    def off(v, d):
        return lax.rem(v + (d + 4), 4)

    def nb(axis, d):
        q = dict(pos)
        q[axis] = off(q[axis], d)
        return dev(q["x"], q["y"], q["z"], c)

    sibling = dev(x, y, z, 1 - c)

    def rc(src, dst, ss, rs, to):
        return pltpu.make_async_remote_copy(
            src_ref=src, dst_ref=dst, send_sem=ss, recv_sem=rs, device_id=to, device_id_type=MESH)

    def block_index(o, axis_idx, rows):
        lo, hi = ROWS[o]
        if rows is None:
            rows = (lo, hi)
        return (axis_idx["z"], axis_idx["y"], axis_idx["x"], slice(*rows))

    def grid_index(o, lead, k):
        axes = ORDERS[o]
        idx = {a: pos[a] for a in axes[:lead]}
        idx[axes[lead]] = k
        for a in axes[lead + 1:]:
            idx[a] = ALL
        return block_index(o, idx, None)

    def vidx(r, cc, g):
        return (r, g[0], cc, g[1], g[2], g[3], ALL)

    def ag_copy(r, o, p, d):
        lead = 2 - p
        axis = ORDERS[o][lead]
        i = ((r * 3 + o) * 3 + p) * 3 + d - 1
        ref = V.at[vidx(r, c, grid_index(o, lead, pos[axis]))]
        return rc(ref, ref, ag_s.at[i], ag_r.at[i], nb(axis, d))

    def fw_copy(r, o, d):
        me = pos[ORDERS[o][0]]
        ref = V.at[vidx(r, c, grid_index(o, 0, off(me, -d)))]
        i = (r * 3 + o) * 4 + d
        return rc(ref, ref, fw_s.at[i], fw_r.at[i], sibling)

    def ag_start(r, p, ds=(1, 3, 2)):
        for d in ds:
            for o in range(3):
                ag_copy(r, o, p, d).start()

    def fw_own(r):
        for o in range(3):
            fw_copy(r, o, 0).start()

    def ag_finish(r, p, ds=(1, 3, 2)):
        for d in ds:
            for o in range(3):
                ag_copy(r, o, p, d).wait_recv()
                if p == 2:
                    fw_copy(r, o, d).start()

    def fw_wait(r):
        for o in range(3):
            for d in range(4):
                fw_copy(r, o, d).wait_recv()

    def ag_sent(r):
        for o in range(3):
            for p in range(3):
                for d in (1, 2, 3):
                    ag_copy(r, o, p, d).wait_send()
            for d in range(4):
                fw_copy(r, o, d).wait_send()

    def u_copy(k):
        i, to, rows = ((x, nb("x", 1), ALL), (x, nb("x", -1), ALL),
                       (off(x, -1), nb("x", 1), slice(0, 16)), (off(x, 1), nb("x", -1), slice(16, 32)))[k]
        ref = utg.at[c, i, rows, :]
        return rc(ref, ref, u_s.at[k], u_r.at[k], to)

    def u_sib():
        return rc(utg.at[c], utg.at[c], u_s.at[4], u_r.at[4], sibling)

    def e_sib():
        return rc(eg.at[c], eg.at[c], e_s.at[3], e_r.at[3], sibling)

    def e_copy(d):
        xt = off(x, d)
        cols = pl.ds(pl.multiple_of(xt * 128, 128), 128)
        return rc(eig.at[:, cols], eg.at[c, x], e_s.at[d - 1], e_r.at[d - 1], dev(xt, y, z, c))

    def sb_copy(s, zi):
        return rc(V.at[s, zi, 1 - c], sib.at[s, zi], sb_s.at[s * 4 + zi], sb_r.at[s * 4 + zi], sibling)

    def rs_copy(s, o, p, d):
        axis = ORDERS[o][p]
        i = ((s * 3 + o) * 3 + p) * 3 + d - 1
        g = grid_index(o, p, off(pos[axis], d))
        return rc(V.at[vidx(s, c, g)], RF[o][p].at[s, d - 1], rs_s.at[i], rs_r.at[i], nb(axis, d))

    def rs_start(s, p):
        for d in (2, 1, 3):
            for o in range(3):
                rs_copy(s, o, p, d).start()

    def rs_end(s, p):
        for o in range(3):
            for d in (1, 3, 2):
                rs_copy(s, o, p, d).wait_recv()
            v = vidx(s, c, grid_index(o, p, pos[ORDERS[o][p]]))
            V[v] = (V[v] + RF[o][p][s, 0]) + (RF[o][p][s, 1] + RF[o][p][s, 2])

    def push(s, zi):
        sb_copy(s, zi).wait_recv()
        for yi in range(4):
            V[s, zi, c, yi] = V[s, zi, c, yi] + sib[s, zi, yi]
        dz = off(zi - z, 4)

        @pl.when(dz != 0)
        def _():
            rs_copy(s, 0, 0, dz).start()
        for d in (2, 1, 3):
            i = (s * 3 + 1) * 9 + d - 1
            lo, hi = ROWS[1]
            rc(V.at[s, zi, c, off(y, d), :, lo:hi, :], RF[1][0].at[s, d - 1, zi],
               rs_s.at[i], rs_r.at[i], nb("y", d)).start()
            i = (s * 3 + 2) * 9 + d - 1
            lo, hi = ROWS[2]
            rc(V.at[s, zi, c, :, off(x, d), lo:hi, :], RF[2][0].at[s, d - 1, zi],
               rs_s.at[i], rs_r.at[i], nb("x", d)).start()

    def peer(k):
        return off(y, 0 + lax.div(k, 4)), off(z, 0 + lax.rem(k, 4))

    def mg_copy(s, k):
        yt, zt = peer(k)
        i = s * 16 + k
        return rc(V.at[s, z, c, y, x], mg.at[s, y, z], mg_s.at[i], mg_r.at[i], dev(x, yt, zt, c))

    def ub_copy(s, k):
        yt, zt = peer(k)
        i = s * 16 + k
        return rc(ub.at[s, yt, zt], rb.at[s, k], ub_s.at[i], ub_r.at[i], dev(x, yt, zt, c))

    def column_peer(k):
        xt = off(x, lax.div(k, 4))
        lt = lax.rem(ylo + lax.rem(lax.div(k, 2), 2), 2)
        ct = lax.rem(c + lax.rem(k, 2), 2)
        return dev(xt, yhi * 2 + lt, z, ct), ct

    def ud_copy(s, k):
        to, ct = column_peer(k)
        i = s * 16 + k
        rows = pl.ds(pl.multiple_of(ct * 32, 32), 32)
        return rc(us.at[s, rows, :], ud.at[s, x, ylo, c], ud_s.at[i], ud_r.at[i], to)

    def loop(lo, hi, f):
        def step(i, carry):
            f(i)
            return carry
        lax.fori_loop(lo, hi, step, 0)

    def t_copy(j, slot):
        cols = pl.ds(pl.multiple_of(j * 256, 256), 256)
        return pltpu.make_async_copy(tok.at[:, cols], stage.at[slot], st_sem.at[slot])

    t_copy(0, 0).start()
    t_copy(1, 1).start()
    val_copies = []
    rowbase = pl.multiple_of(x * 64, 64)
    colbase = pl.multiple_of(ylo * 128, 128)
    for r in range(2):
        cols = pl.ds(pl.multiple_of(colbase + r * 256, 128), 128)
        val_copies.append(pltpu.make_async_copy(
            val.at[pl.ds(rowbase, 64), cols], V.at[r, z, c, y, x], lc_sem.at[r]))
        val_copies[-1].start()
    cv_copy = pltpu.make_async_copy(curv, cv, lc_sem.at[2])
    cv_copy.start()
    ut_copy = pltpu.make_async_copy(ut, utg.at[c, x], lc_sem.at[3])
    ut_copy.start()
    ob_copy = pltpu.make_async_copy(outb_hbm, outb, lc_sem.at[4])
    ob_copy.start()

    barrier = pltpu.get_barrier_semaphore()
    loop(1, 16, lambda k: pl.semaphore_signal(
        barrier, inc=1, device_id=dev(x, *peer(k), c), device_id_type=MESH))

    def greet(k):
        pl.semaphore_signal(barrier, inc=1, device_id=column_peer(k)[0], device_id_type=MESH)
    greet(1)
    loop(3, 16, greet)
    pl.semaphore_wait(barrier, 29)

    for cp in val_copies:
        cp.wait()

    def split_block(j):
        slot = lax.rem(j, 2)
        t_copy(j, slot).wait()
        kb = lax.div(j, 2)
        cols = pl.ds(pl.multiple_of(lax.rem(j, 2) * 256, 256), 256)

        def rows(i):
            rr = pl.ds(pl.multiple_of(i * 256, 256), 256)
            h, l = split(stage[slot, rr, :])
            thi[kb, rr, cols] = h
            tlo[kb, rr, cols] = l
        loop(0, 4, rows)

        @pl.when(j < 14)
        def _():
            t_copy(j + 2, slot).start()

    ag_start(0, 0)
    ag_start(1, 0)
    loop(0, 3, split_block)
    ag_finish(0, 0)
    ag_start(0, 1)
    ag_finish(1, 0)
    ag_start(1, 1)
    loop(3, 7, split_block)
    ag_finish(0, 1)
    ag_start(0, 2)
    fw_own(0)
    loop(7, 12, split_block)
    ag_finish(1, 1)
    ob_copy.wait()
    turned = outb[...].T.reshape(8, 2, 32, 512)
    for s in range(2):
        h, l = split(turned[:, s].reshape(256, 512))
        oth[s * 256:(s + 1) * 256, :] = h
        otl[s * 256:(s + 1) * 256, :] = l
    ut_copy.wait()
    for d in (1, 2, 3):
        e_copy(d).start()
    eg[c, x] = eig[:, pl.ds(pl.multiple_of(x * 128, 128), 128)]
    loop(12, 16, split_block)
    cv_copy.wait()
    ag_finish(0, 2, (1, 3))
    ag_start(1, 2, (1, 3))
    fw_own(1)
    ag_finish(0, 2, (2,))
    ag_start(1, 2, (2,))
    fw_wait(0)

    def project(r, steps):
        def body(kb):
            for at, fn in steps:
                pl.when(kb == at)(fn)
            yh, zi = lax.div(kb, 4), lax.rem(kb, 4)
            rows = []
            for ci in range(2):
                tiles = [V[r, zi, ci, yh * 2 + yl].reshape(256, 128) for yl in range(2)]
                rows.append(jnp.concatenate(tiles, axis=1))
            vh, vl = split(jnp.concatenate(rows, axis=0))
            for m in range(2):
                rr = slice(m * 512, (m + 1) * 512)
                acc[rr, :] = acc[rr, :] + mm3(thi[kb, rr, :], tlo[kb, rr, :], vh, vl)
        acc[...] = jnp.zeros_like(acc)
        loop(0, 8, body)

        def weigh(i):
            rr = pl.ds(pl.multiple_of(i * 256, 256), 256)
            cols = slice(r * 256, (r + 1) * 256)
            h, l = split(cv[rr, cols] * acc[rr, :] * inverse_total)
            whi[rr, cols] = h
            wlo[rr, cols] = l
        loop(0, 4, weigh)

    def u_relay():
        u_copy(0).wait_recv()
        u_copy(2).start()
        u_copy(1).wait_recv()
        u_copy(3).start()

    project(0, [(6, lambda: ag_finish(1, 2, (1, 3)))])
    ag_finish(1, 2, (2,))
    for d in (1, 2, 3):
        e_copy(d).wait_recv()
    e_sib().start()
    u_copy(0).start()
    u_copy(1).start()
    fw_wait(1)
    project(1, [])
    ag_sent(0)
    ag_sent(1)

    def z_part(i):
        rr = pl.ds(pl.multiple_of(i * 256, 256), 256)
        h, l = split(mm3(oth[...], otl[...], whi[rr, :], wlo[rr, :], NT))
        zhi[:, rr] = h
        zlo[:, rr] = l
    loop(0, 4, z_part)

    def moment(s, steps):
        def body(i):
            for at, fn in steps:
                pl.when(i == at)(fn)
            zi, yh = lax.div(i, 2), lax.rem(i, 2)
            kb = yh * 4 + zi
            zr = slice(s * 256, (s + 1) * 256)
            mo = mm3(zhi[zr, :], zlo[zr, :], thi[kb], tlo[kb]).reshape(4, 2, 32, 512)
            for cj in range(2):
                for cr in range(2):
                    for yl in range(2):
                        q = (cr * 2 + yl) * 128
                        V[s, zi, cj, yh * 2 + yl, :, cr * 32:(cr + 1) * 32, :] = mo[:, cj, :, q:q + 128]

            @pl.when(yh == 1)
            def _():
                sb_copy(s, zi).start()

            @pl.when((yh == 1) & (zi > 0))
            def _():
                push(s, zi - 1)
        loop(0, 8, body)

    moment(0, [(4, u_relay)])

    def u_share():
        u_copy(2).wait_recv()
        u_copy(3).wait_recv()
        u_sib().start()

    moment(1, [(1, lambda: push(0, 3))])

    def mg_send(s):
        mg[s, y, z] = V[s, z, c, y, x]
        loop(1, 16, lambda k: mg_copy(s, k).start())

    def rotate(s):
        loop(1, 16, lambda k: mg_copy(s, k).wait_recv())
        total = jnp.zeros((32, 256), F32)
        for kb in range(8):
            yh, zi = kb // 4, kb % 4
            lhs = jnp.concatenate(
                [mg[s, yh * 2 + yl, zi, cr * 32:(cr + 1) * 32] for cr in range(2) for yl in range(2)], axis=1)
            lh, ll = split(lhs)
            cols = slice(kb * 512, (kb + 1) * 512)
            both = mm(jnp.concatenate([lh, ll], axis=0), uhi[:, cols], NT)
            total = total + (both[:32] + (both[32:] + mm(lh, ulo[:, cols], NT)))
        sh, sl = split(total / et[pl.ds(pl.multiple_of(c * 64 + s * 32, 32), 32), :])
        for kb in range(8):
            yh, zi = kb // 4, kb % 4
            cols = slice(kb * 512, (kb + 1) * 512)
            both = mm(jnp.concatenate([sh, sl], axis=0), uhi[:, cols])
            part = both[:32] + (both[32:] + mm(sh, ulo[:, cols]))
            for cr in range(2):
                for yl in range(2):
                    q = (cr * 2 + yl) * 128
                    ub[s, yh * 2 + yl, zi, cr * 32:(cr + 1) * 32] = part[:, q:q + 128]
        loop(1, 16, lambda k: ub_copy(s, k).start())

    def ud_send(s):
        loop(1, 16, lambda k: ub_copy(s, k).wait_recv())
        total = ub[s, y, z]
        for k in range(1, 16):
            total = total + rb[s, k]
        us[s] = total
        loop(1, 16, lambda k: ud_copy(s, k).start())
        ud[s, x, ylo, c] = us[s, pl.ds(pl.multiple_of(c * 32, 32), 32), :]

    push(1, 3)
    rs_end(0, 0)
    rs_start(0, 1)
    u_share()
    rs_end(1, 0)
    rs_start(1, 1)
    rs_end(0, 1)
    rs_start(0, 2)
    rs_end(1, 1)
    rs_start(1, 2)
    rs_end(0, 2)
    mg_send(0)
    rs_end(1, 2)
    mg_send(1)
    u_sib().wait_recv()
    for ci in range(2):
        for i in range(4):
            rr = slice((ci * 4 + i) * 32, (ci * 4 + i + 1) * 32)
            h, l = split(utg[ci, i])
            uhi[rr, :] = h
            ulo[rr, :] = l
    e_sib().wait_recv()
    et[...] = eg[...].reshape(256, 128).T
    rotate(0)
    rotate(1)
    ud_send(0)
    ud_send(1)
    oh, ol = split(outb[...])
    for s in range(2):
        loop(1, 16, lambda k: ud_copy(s, k).wait_recv())
    cols = []
    for yl in range(2):
        cols.append(jnp.concatenate([ud[s, xi, yl, ci] for xi in range(4) for ci in range(2) for s in range(2)], axis=0))
    dh, dl = split(jnp.concatenate(cols, axis=1))
    out[...] = mm3(oh, ol, dh, dl).T

    for k in range(4):
        u_copy(k).wait_send()
    u_sib().wait_send()
    e_sib().wait_send()
    for d in (1, 2, 3):
        e_copy(d).wait_send()
    for s in range(2):
        loop(0, 4, lambda zi: sb_copy(s, zi).wait_send())
        for o in range(3):
            for p in range(3):
                for d in (1, 2, 3):
                    rs_copy(s, o, p, d).wait_send()
        for f in (mg_copy, ub_copy, ud_copy):
            loop(1, 16, lambda k: f(s, k).wait_send())


def body(tokens, curvature, values, input_basis, output_basis, eigenvalues):
    inverse_total = 1.0 / (tokens.shape[0] * lax.axis_size("dp") * lax.axis_size("fsdp"))
    dma = pltpu.SemaphoreType.DMA
    scratch = [
        pltpu.VMEM((2, 4, 2, 4, 4, 64, 128), F32),
        pltpu.VMEM((8, 1024, 512), BF16),
        pltpu.VMEM((8, 1024, 512), BF16),
        pltpu.VMEM((2, 1024, 256), F32),
        pltpu.VMEM((1024, 512), F32),
        pltpu.VMEM((1024, 256), F32),
        pltpu.VMEM((1024, 512), BF16),
        pltpu.VMEM((1024, 512), BF16),
        pltpu.VMEM((512, 1024), BF16),
        pltpu.VMEM((512, 1024), BF16),
        pltpu.VMEM((2, 4, 4, 4, 64, 128), F32),
        pltpu.VMEM((2, 4, 4, 64, 128), F32),
        pltpu.VMEM((2, 4, 32, 4096), F32),
        pltpu.VMEM((256, 4096), BF16),
        pltpu.VMEM((256, 4096), BF16),
        pltpu.VMEM((2, 4, 32, 128), F32),
        pltpu.VMEM((128, 256), F32),
        pltpu.VMEM((2, 4, 4, 64, 128), F32),
        pltpu.VMEM((2, 16, 64, 128), F32),
        pltpu.VMEM((2, 64, 128), F32),
        pltpu.VMEM((2, 4, 2, 2, 32, 128), F32),
        pltpu.VMEM((512, 512), F32),
        pltpu.VMEM((512, 512), BF16),
        pltpu.VMEM((512, 512), BF16),
    ]
    scratch += [pltpu.VMEM((2, 3) + full_shape(o, p), F32) for o in range(3) for p in range(3)]
    for n in (54, 54, 24, 24, 5, 5, 4, 4, 8, 8, 54, 54, 32, 32, 32, 32, 32, 32, 2, 5):
        scratch.append(dma((n,)))
    hbm = pl.BlockSpec(memory_space=pl.ANY)
    vmem = pl.BlockSpec(memory_space=pltpu.VMEM)
    update = pl.pallas_call(
        functools.partial(kernel, inverse_total=inverse_total),
        out_shape=jax.ShapeDtypeStruct((256, 512), F32),
        in_specs=[hbm, hbm, hbm, hbm, hbm, vmem],
        out_specs=vmem,
        scratch_shapes=scratch,
        compiler_params=pltpu.CompilerParams(
            collective_id=0, has_side_effects=True, vmem_limit_bytes=63 * 1024 * 1024
        ),
        cost_estimate=pl.CostEstimate(flops=30_000_000_000, bytes_accessed=24_000_000, transcendentals=0),
    )(
        tokens,
        curvature,
        values,
        input_basis.T,
        output_basis,
        eigenvalues,
    )
    return values - update


def solution(mesh):
    placed = (
        P(("dp", "fsdp"), None),
        P(("dp", "fsdp"), None),
        P("fsdp", None),
        P(None, ("dp", "fsdp")),
        P(),
        P(("dp", "fsdp"), None),
    )
    return jax.shard_map(
        body, mesh=mesh, in_specs=placed, out_specs=P("fsdp", None), check_vma=False
    )
```

```python
import functools

import jax
import jax.numpy as jnp
from jax import lax
from jax.experimental import pallas as pl
from jax.experimental.pallas import tpu as pltpu
from jax.sharding import PartitionSpec as P

F32 = jnp.float32
BF16 = jnp.bfloat16
MESH = pl.DeviceIdType.MESH
ALL = slice(None)

ORDERS = (("z", "y", "x"), ("y", "x", "z"), ("x", "z", "y"))
ROWS = ((0, 24), (24, 48), (48, 64))


def split(v):
    hi = v.astype(BF16)
    return hi, (v - hi.astype(F32)).astype(BF16)


def mm(a, b, dims=(((1,), (0,)), ((), ()))):
    return lax.dot_general(a, b, dims, preferred_element_type=F32)


NT = (((1,), (1,)), ((), ()))


def mm3(ah, al, bh, bl, dims=(((1,), (0,)), ((), ()))):
    return mm(ah, bh, dims) + (mm(ah, bl, dims) + mm(al, bh, dims))


def full_shape(o, p):
    lo, hi = ROWS[o]
    return ((4, 4), (4,), ())[p] + (hi - lo, 128)


def kernel(tok, curv, val, ut, outb_hbm, eig, out, *scr, inverse_total):
    (V, thi, tlo, stage, cv, acc, whi, wlo, zhi, zlo, sib, mg, utg, uhi, ulo, eg, et, ub, rba, rbb, us, ud,
     outb, oth, otl, vall, *rest) = scr
    RF = [[rest[o * 3 + p] for p in range(3)] for o in range(3)]
    (ag_s, ag_r, fw_s, fw_r, u_s, u_r, e_s, e_r, sb_s, sb_r, rs_s, rs_r,
     mg_s, mg_r, ub_s, ub_r, ud_s, ud_r, st_sem, lc_sem) = rest[9:]

    dp = lax.axis_index("dp")
    fs = lax.axis_index("fsdp")
    x, ylo = lax.div(dp, 2), lax.rem(dp, 2)
    yhi, z, c = lax.div(fs, 8), lax.rem(lax.div(fs, 2), 4), lax.rem(fs, 2)
    y = yhi * 2 + ylo
    pos = {"x": x, "y": y, "z": z}

    def dev(x_, y_, z_, c_):
        return (x_ * 2 + lax.rem(y_, 2), lax.div(y_, 2) * 8 + z_ * 2 + c_)

    def off(v, d):
        return lax.rem(v + (d + 4), 4)

    def nb(axis, d):
        q = dict(pos)
        q[axis] = off(q[axis], d)
        return dev(q["x"], q["y"], q["z"], c)

    sibling = dev(x, y, z, 1 - c)

    def rc(src, dst, ss, rs, to):
        return pltpu.make_async_remote_copy(
            src_ref=src, dst_ref=dst, send_sem=ss, recv_sem=rs, device_id=to, device_id_type=MESH)

    def block_index(o, axis_idx, rows):
        lo, hi = ROWS[o]
        if rows is None:
            rows = (lo, hi)
        return (axis_idx["z"], axis_idx["y"], axis_idx["x"], slice(*rows))

    def grid_index(o, lead, k):
        axes = ORDERS[o]
        idx = {a: pos[a] for a in axes[:lead]}
        idx[axes[lead]] = k
        for a in axes[lead + 1:]:
            idx[a] = ALL
        return block_index(o, idx, None)

    def vidx(r, cc, g):
        return (r, g[0], cc, g[1], g[2], g[3], ALL)

    def ag_copy(r, o, p, d):
        lead = 2 - p
        axis = ORDERS[o][lead]
        i = ((r * 3 + o) * 3 + p) * 3 + d - 1
        ref = V.at[vidx(r, c, grid_index(o, lead, pos[axis]))]
        return rc(ref, ref, ag_s.at[i], ag_r.at[i], nb(axis, d))

    def fw_copy(r, o, d):
        me = pos[ORDERS[o][0]]
        ref = V.at[vidx(r, c, grid_index(o, 0, off(me, -d)))]
        i = (r * 3 + o) * 4 + d
        return rc(ref, ref, fw_s.at[i], fw_r.at[i], sibling)

    def ag_start(r, p, ds=(1, 3, 2)):
        for d in ds:
            for o in range(3):
                ag_copy(r, o, p, d).start()

    def fw_own(r):
        for o in range(3):
            fw_copy(r, o, 0).start()

    def ag_finish(r, p, ds=(1, 3, 2)):
        for d in ds:
            for o in range(3):
                ag_copy(r, o, p, d).wait_recv()
                if p == 2:
                    fw_copy(r, o, d).start()

    def fw_wait(r):
        for o in range(3):
            for d in range(4):
                fw_copy(r, o, d).wait_recv()

    def ag_sent(r):
        for o in range(3):
            for p in range(3):
                for d in (1, 2, 3):
                    ag_copy(r, o, p, d).wait_send()
            for d in range(4):
                fw_copy(r, o, d).wait_send()

    def u_copy(k):
        i, to, rows = ((x, nb("x", 1), ALL), (x, nb("x", -1), ALL),
                       (off(x, -1), nb("x", 1), slice(0, 16)), (off(x, 1), nb("x", -1), slice(16, 32)))[k]
        ref = utg.at[c, i, rows, :]
        return rc(ref, ref, u_s.at[k], u_r.at[k], to)

    def u_sib():
        return rc(utg.at[c], utg.at[c], u_s.at[4], u_r.at[4], sibling)

    def e_sib():
        return rc(eg.at[c], eg.at[c], e_s.at[3], e_r.at[3], sibling)

    def e_copy(d):
        xt = off(x, d)
        cols = pl.ds(pl.multiple_of(xt * 128, 128), 128)
        return rc(eig.at[:, cols], eg.at[c, x], e_s.at[d - 1], e_r.at[d - 1], dev(xt, y, z, c))

    def sb_copy(s, zi):
        return rc(V.at[s, zi, 1 - c], sib.at[s, zi], sb_s.at[s * 4 + zi], sb_r.at[s * 4 + zi], sibling)

    def rs_copy(s, o, p, d):
        axis = ORDERS[o][p]
        i = ((s * 3 + o) * 3 + p) * 3 + d - 1
        g = grid_index(o, p, off(pos[axis], d))
        return rc(V.at[vidx(s, c, g)], RF[o][p].at[s, d - 1], rs_s.at[i], rs_r.at[i], nb(axis, d))

    def rs_start(s, p):
        for d in (2, 1, 3):
            for o in range(3):
                rs_copy(s, o, p, d).start()

    def rs_end(s, p):
        for o in range(3):
            for d in (1, 3, 2):
                rs_copy(s, o, p, d).wait_recv()
            v = vidx(s, c, grid_index(o, p, pos[ORDERS[o][p]]))
            V[v] = (V[v] + RF[o][p][s, 0]) + (RF[o][p][s, 1] + RF[o][p][s, 2])

    def push(s, zi):
        sb_copy(s, zi).wait_recv()
        for yi in range(4):
            V[s, zi, c, yi] = V[s, zi, c, yi] + sib[s, zi, yi]
        dz = off(zi - z, 4)

        @pl.when(dz != 0)
        def _():
            rs_copy(s, 0, 0, dz).start()
        for d in (2, 1, 3):
            i = (s * 3 + 1) * 9 + d - 1
            lo, hi = ROWS[1]
            rc(V.at[s, zi, c, off(y, d), :, lo:hi, :], RF[1][0].at[s, d - 1, zi],
               rs_s.at[i], rs_r.at[i], nb("y", d)).start()
            i = (s * 3 + 2) * 9 + d - 1
            lo, hi = ROWS[2]
            rc(V.at[s, zi, c, :, off(x, d), lo:hi, :], RF[2][0].at[s, d - 1, zi],
               rs_s.at[i], rs_r.at[i], nb("x", d)).start()

    def mg_copy(s, h, step, d):
        rows = slice(h * 32, h * 32 + 32)
        axis = "yz"[h ^ step]
        if step == 0:
            ref = mg.at[s, y, z, rows, :]
        elif h == 0:
            ref = mg.at[s, :, z, rows, :]
        else:
            ref = mg.at[s, y, :, rows, :]
        i = ((s * 2 + h) * 2 + step) * 3 + d - 1
        return rc(ref, ref, mg_s.at[i], mg_r.at[i], nb(axis, d))

    def ub_copy(s, h, step, d):
        rows = slice(h * 32, h * 32 + 32)
        axis = "zy"[h ^ step]
        to = off(pos[axis], d)
        if step == 0:
            src = ub.at[s, :, to, rows, :] if h == 0 else ub.at[s, to, :, rows, :]
            dst = rba.at[s, h, d - 1]
        else:
            src = ub.at[s, to, z, rows, :] if h == 0 else ub.at[s, y, to, rows, :]
            dst = rbb.at[s, h, d - 1]
        i = ((s * 2 + h) * 2 + step) * 3 + d - 1
        return rc(src, dst, ub_s.at[i], ub_r.at[i], nb(axis, d))

    def column_peer(k):
        xt = off(x, lax.div(k, 4))
        lt = lax.rem(ylo + lax.rem(lax.div(k, 2), 2), 2)
        ct = lax.rem(c + lax.rem(k, 2), 2)
        return dev(xt, yhi * 2 + lt, z, ct), ct

    def ud_copy(s, k):
        to, ct = column_peer(k)
        i = s * 16 + k
        rows = pl.ds(pl.multiple_of(ct * 32, 32), 32)
        return rc(us.at[s, rows, :], ud.at[s, x, ylo, c], ud_s.at[i], ud_r.at[i], to)

    def loop(lo, hi, f):
        def step(i, carry):
            f(i)
            return carry
        lax.fori_loop(lo, hi, step, 0)

    def t_copy(j, slot):
        cols = pl.ds(pl.multiple_of(j * 256, 256), 256)
        return pltpu.make_async_copy(tok.at[:, cols], stage.at[slot], st_sem.at[slot])

    t_copy(0, 0).start()
    t_copy(1, 1).start()
    val_copies = []
    rowbase = pl.multiple_of(x * 64, 64)
    colbase = pl.multiple_of(ylo * 128, 128)
    for r in range(2):
        cols = pl.ds(pl.multiple_of(colbase + r * 256, 128), 128)
        val_copies.append(pltpu.make_async_copy(
            val.at[pl.ds(rowbase, 64), cols], V.at[r, z, c, y, x], lc_sem.at[r]))
        val_copies[-1].start()
    cv_copy = pltpu.make_async_copy(curv, cv, lc_sem.at[2])
    cv_copy.start()
    ut_copy = pltpu.make_async_copy(ut, utg.at[c, x], lc_sem.at[3])
    ut_copy.start()
    va_copy = pltpu.make_async_copy(val, vall, lc_sem.at[5])
    va_copy.start()
    ob_copy = pltpu.make_async_copy(outb_hbm, outb, lc_sem.at[4])
    ob_copy.start()

    barrier = pltpu.get_barrier_semaphore()
    for axis in "yz":
        for d in (1, 2, 3):
            pl.semaphore_signal(barrier, inc=1, device_id=nb(axis, d), device_id_type=MESH)

    def greet(k):
        pl.semaphore_signal(barrier, inc=1, device_id=column_peer(k)[0], device_id_type=MESH)
    greet(1)
    loop(3, 16, greet)
    pl.semaphore_wait(barrier, 20)

    for cp in val_copies:
        cp.wait()

    def split_block(j):
        slot = lax.rem(j, 2)
        t_copy(j, slot).wait()
        kb = lax.div(j, 2)
        cols = pl.ds(pl.multiple_of(lax.rem(j, 2) * 256, 256), 256)

        def rows(i):
            rr = pl.ds(pl.multiple_of(i * 256, 256), 256)
            h, l = split(stage[slot, rr, :])
            thi[kb, rr, cols] = h
            tlo[kb, rr, cols] = l
        loop(0, 4, rows)

        @pl.when(j < 14)
        def _():
            t_copy(j + 2, slot).start()

    ag_start(0, 0)
    ag_start(1, 0)
    loop(0, 3, split_block)
    ag_finish(0, 0)
    ag_start(0, 1)
    ag_finish(1, 0)
    ag_start(1, 1)
    loop(3, 7, split_block)
    ag_finish(0, 1)
    ag_start(0, 2)
    fw_own(0)
    loop(7, 12, split_block)
    ag_finish(1, 1)
    ob_copy.wait()
    turned = outb[...].T.reshape(8, 2, 32, 512)
    for s in range(2):
        h, l = split(turned[:, s].reshape(256, 512))
        oth[s * 256:(s + 1) * 256, :] = h
        otl[s * 256:(s + 1) * 256, :] = l
    ut_copy.wait()
    for d in (1, 2, 3):
        e_copy(d).start()
    eg[c, x] = eig[:, pl.ds(pl.multiple_of(x * 128, 128), 128)]
    loop(12, 16, split_block)
    cv_copy.wait()
    ag_finish(0, 2, (1, 3))
    ag_start(1, 2, (1, 3))
    fw_own(1)
    ag_finish(0, 2, (2,))
    ag_start(1, 2, (2,))
    fw_wait(0)

    def project(r, steps):
        def body(kb):
            for at, fn in steps:
                pl.when(kb == at)(fn)
            parts = []
            for kk in range(2):
                k2 = kb * 2 + kk
                yh, zi = lax.div(k2, 4), lax.rem(k2, 4)
                rows = []
                for ci in range(2):
                    tiles = [V[r, zi, ci, yh * 2 + yl].reshape(256, 128) for yl in range(2)]
                    rows.append(jnp.concatenate(tiles, axis=1))
                parts.append(split(jnp.concatenate(rows, axis=0)))
            for m in range(2):
                rr = slice(m * 512, (m + 1) * 512)
                part = acc[rr, :]
                for kk, (vh, vl) in enumerate(parts):
                    part = part + mm3(thi[kb * 2 + kk, rr, :], tlo[kb * 2 + kk, rr, :], vh, vl)
                acc[rr, :] = part
        acc[...] = jnp.zeros_like(acc)
        loop(0, 4, body)

        def weigh(i):
            rr = pl.ds(pl.multiple_of(i * 256, 256), 256)
            cols = slice(r * 256, (r + 1) * 256)
            h, l = split(cv[rr, cols] * acc[rr, :] * inverse_total)
            whi[rr, cols] = h
            wlo[rr, cols] = l
        loop(0, 4, weigh)

    def u_relay():
        u_copy(0).wait_recv()
        u_copy(2).start()
        u_copy(1).wait_recv()
        u_copy(3).start()

    project(0, [(3, lambda: ag_finish(1, 2, (1, 3)))])
    ag_finish(1, 2, (2,))
    for d in (1, 2, 3):
        e_copy(d).wait_recv()
    e_sib().start()
    u_copy(0).start()
    u_copy(1).start()
    fw_wait(1)
    project(1, [])
    ag_sent(0)
    ag_sent(1)

    def z_part(i):
        rr = pl.ds(pl.multiple_of(i * 256, 256), 256)
        both = mm(jnp.concatenate([oth[...], otl[...]], axis=0), whi[rr, :], NT)
        h, l = split(both[:512] + (both[512:] + mm(oth[...], wlo[rr, :], NT)))
        zhi[:, rr] = h
        zlo[:, rr] = l
    loop(0, 4, z_part)

    def moment(s, steps):
        def body(i):
            for at, fn in steps:
                pl.when(i == at)(fn)
            zi, yh = lax.div(i, 2), lax.rem(i, 2)
            kb = yh * 4 + zi
            zr = slice(s * 256, (s + 1) * 256)
            both = mm(jnp.concatenate([zhi[zr, :], zlo[zr, :]], axis=0), thi[kb])
            mo = (both[:256] + (both[256:] + mm(zhi[zr, :], tlo[kb]))).reshape(4, 2, 32, 512)
            for cj in range(2):
                for cr in range(2):
                    for yl in range(2):
                        q = (cr * 2 + yl) * 128
                        V[s, zi, cj, yh * 2 + yl, :, cr * 32:(cr + 1) * 32, :] = mo[:, cj, :, q:q + 128]

            @pl.when(yh == 1)
            def _():
                sb_copy(s, zi).start()

            @pl.when((yh == 1) & (zi > 0))
            def _():
                push(s, zi - 1)
        loop(0, 8, body)

    moment(0, [(4, u_relay)])

    def u_share():
        u_copy(2).wait_recv()
        u_copy(3).wait_recv()
        u_sib().start()

    moment(1, [(1, lambda: push(0, 3))])

    def mg_send(s):
        mg[s, y, z] = V[s, z, c, y, x]
        for h in range(2):
            for d in (2, 1, 3):
                mg_copy(s, h, 0, d).start()

    def mg_mid(s):
        for h in range(2):
            for d in (1, 3, 2):
                mg_copy(s, h, 0, d).wait_recv()
            for d in (2, 1, 3):
                mg_copy(s, h, 1, d).start()

    def rotate(s):
        for h in range(2):
            for d in (1, 3, 2):
                mg_copy(s, h, 1, d).wait_recv()
        total = jnp.zeros((32, 256), F32)
        for kb in range(8):
            yh, zi = kb // 4, kb % 4
            lhs = jnp.concatenate(
                [mg[s, yh * 2 + yl, zi, cr * 32:(cr + 1) * 32] for cr in range(2) for yl in range(2)], axis=1)
            lh, ll = split(lhs)
            cols = slice(kb * 512, (kb + 1) * 512)
            both = mm(jnp.concatenate([lh, ll], axis=0), uhi[:, cols], NT)
            total = total + (both[:32] + (both[32:] + mm(lh, ulo[:, cols], NT)))
        sh, sl = split(total / et[pl.ds(pl.multiple_of(c * 64 + s * 32, 32), 32), :])
        for kb in range(8):
            yh, zi = kb // 4, kb % 4
            cols = slice(kb * 512, (kb + 1) * 512)
            both = mm(jnp.concatenate([sh, sl], axis=0), uhi[:, cols])
            part = both[:32] + (both[32:] + mm(sh, ulo[:, cols]))
            for cr in range(2):
                for yl in range(2):
                    q = (cr * 2 + yl) * 128
                    ub[s, yh * 2 + yl, zi, cr * 32:(cr + 1) * 32] = part[:, q:q + 128]
        for h in range(2):
            for d in (2, 1, 3):
                ub_copy(s, h, 0, d).start()

    def ub_mid(s):
        for h in range(2):
            rows = slice(h * 32, h * 32 + 32)
            for d in (1, 3, 2):
                ub_copy(s, h, 0, d).wait_recv()
            v = (s, ALL, z, rows, ALL) if h == 0 else (s, y, ALL, rows, ALL)
            ub[v] = (ub[v] + rba[s, h, 0]) + (rba[s, h, 1] + rba[s, h, 2])
            for d in (2, 1, 3):
                ub_copy(s, h, 1, d).start()

    def ud_send(s):
        for h in range(2):
            rows = slice(h * 32, h * 32 + 32)
            for d in (1, 3, 2):
                ub_copy(s, h, 1, d).wait_recv()
            us[s, rows, :] = (ub[s, y, z, rows, :] + rbb[s, h, 0]) + (rbb[s, h, 1] + rbb[s, h, 2])
        loop(1, 16, lambda k: ud_copy(s, k).start())
        ud[s, x, ylo, c] = us[s, pl.ds(pl.multiple_of(c * 32, 32), 32), :]

    push(1, 3)
    rs_end(0, 0)
    rs_start(0, 1)
    u_share()
    rs_end(1, 0)
    rs_start(1, 1)
    rs_end(0, 1)
    rs_start(0, 2)
    rs_end(1, 1)
    rs_start(1, 2)
    rs_end(0, 2)
    mg_send(0)
    rs_end(1, 2)
    mg_send(1)
    mg_mid(0)
    mg_mid(1)
    u_sib().wait_recv()
    for ci in range(2):
        for i in range(4):
            rr = slice((ci * 4 + i) * 32, (ci * 4 + i + 1) * 32)
            h, l = split(utg[ci, i])
            uhi[rr, :] = h
            ulo[rr, :] = l
    e_sib().wait_recv()
    et[...] = eg[...].reshape(256, 128).T
    rotate(0)
    rotate(1)
    ub_mid(0)
    ub_mid(1)
    ud_send(0)
    ud_send(1)
    oh, ol = split(outb[...])
    for s in range(2):
        loop(1, 16, lambda k: ud_copy(s, k).wait_recv())
    cols = []
    for yl in range(2):
        cols.append(jnp.concatenate([ud[s, xi, yl, ci] for xi in range(4) for ci in range(2) for s in range(2)], axis=0))
    dh, dl = split(jnp.concatenate(cols, axis=1))
    va_copy.wait()
    out[...] = vall[...] - mm3(oh, ol, dh, dl).T

    for k in range(4):
        u_copy(k).wait_send()
    u_sib().wait_send()
    e_sib().wait_send()
    for d in (1, 2, 3):
        e_copy(d).wait_send()
    for s in range(2):
        loop(0, 4, lambda zi: sb_copy(s, zi).wait_send())
        for o in range(3):
            for p in range(3):
                for d in (1, 2, 3):
                    rs_copy(s, o, p, d).wait_send()
        for h in range(2):
            for step in range(2):
                for d in (1, 2, 3):
                    mg_copy(s, h, step, d).wait_send()
                    ub_copy(s, h, step, d).wait_send()
        loop(1, 16, lambda k: ud_copy(s, k).wait_send())


def body(tokens, curvature, values, input_basis, output_basis, eigenvalues):
    inverse_total = 1.0 / (tokens.shape[0] * lax.axis_size("dp") * lax.axis_size("fsdp"))
    dma = pltpu.SemaphoreType.DMA
    scratch = [
        pltpu.VMEM((2, 4, 2, 4, 4, 64, 128), F32),
        pltpu.VMEM((8, 1024, 512), BF16),
        pltpu.VMEM((8, 1024, 512), BF16),
        pltpu.VMEM((2, 1024, 256), F32),
        pltpu.VMEM((1024, 512), F32),
        pltpu.VMEM((1024, 256), F32),
        pltpu.VMEM((1024, 512), BF16),
        pltpu.VMEM((1024, 512), BF16),
        pltpu.VMEM((512, 1024), BF16),
        pltpu.VMEM((512, 1024), BF16),
        pltpu.VMEM((2, 4, 4, 4, 64, 128), F32),
        pltpu.VMEM((2, 4, 4, 64, 128), F32),
        pltpu.VMEM((2, 4, 32, 4096), F32),
        pltpu.VMEM((256, 4096), BF16),
        pltpu.VMEM((256, 4096), BF16),
        pltpu.VMEM((2, 4, 32, 128), F32),
        pltpu.VMEM((128, 256), F32),
        pltpu.VMEM((2, 4, 4, 64, 128), F32),
        pltpu.VMEM((2, 2, 3, 4, 32, 128), F32),
        pltpu.VMEM((2, 2, 3, 32, 128), F32),
        pltpu.VMEM((2, 64, 128), F32),
        pltpu.VMEM((2, 4, 2, 2, 32, 128), F32),
        pltpu.VMEM((512, 512), F32),
        pltpu.VMEM((512, 512), BF16),
        pltpu.VMEM((512, 512), BF16),
        pltpu.VMEM((256, 512), F32),
    ]
    scratch += [pltpu.VMEM((2, 3) + full_shape(o, p), F32) for o in range(3) for p in range(3)]
    for n in (54, 54, 24, 24, 5, 5, 4, 4, 8, 8, 54, 54, 32, 32, 32, 32, 32, 32, 2, 6):
        scratch.append(dma((n,)))
    hbm = pl.BlockSpec(memory_space=pl.ANY)
    vmem = pl.BlockSpec(memory_space=pltpu.VMEM)
    return pl.pallas_call(
        functools.partial(kernel, inverse_total=inverse_total),
        out_shape=jax.ShapeDtypeStruct((256, 512), F32),
        in_specs=[hbm, hbm, hbm, hbm, hbm, vmem],
        out_specs=vmem,
        scratch_shapes=scratch,
        compiler_params=pltpu.CompilerParams(
            collective_id=0, has_side_effects=True, vmem_limit_bytes=63 * 1024 * 1024
        ),
        cost_estimate=pl.CostEstimate(flops=30_000_000_000, bytes_accessed=24_000_000, transcendentals=0),
    )(
        tokens,
        curvature,
        values,
        input_basis.T,
        output_basis,
        eigenvalues,
    )


def solution(mesh):
    placed = (
        P(("dp", "fsdp"), None),
        P(("dp", "fsdp"), None),
        P("fsdp", None),
        P(None, ("dp", "fsdp")),
        P(),
        P(("dp", "fsdp"), None),
    )
    return jax.shard_map(
        body, mesh=mesh, in_specs=placed, out_specs=P("fsdp", None), check_vma=False
    )
```
